32 devices in a mesh: ctx: 8 (over z, y), head: 4 (over x, core).
Axes of the slice: x: 2, y: 2, z: 4, core: 2. Of those that a mesh axis runs over, the one named last changes fastest.
Arguments:
- queries: bfloat16 [1024, 4096], P('ctx', 'head'), may hold values from -30 to 30
- key_proj: bfloat16 [1024, 1024], P('ctx', 'head'), may hold values from -6 to 6
- value_proj: bfloat16 [1024, 1024], P('ctx', 'head'), may hold values from -6 to 6
- lengths: int32 [8], replicated, may hold values from 1 to 512, 1024 in all
- out_weight: bfloat16 [4096, 8192], P(None, 'head'), may hold values from -0.09375 to 0.09375
Outputs:
- mixed_out: bfloat16 [1024, 8192], P('ctx', 'head')
The draws below stay inside these ranges and needn't reach their ends.
Inputs may be any that keep to these rules, and one draw needn't show every extreme that they name: Document lengths in pack order; they sum to 1024 and the longest is exactly 512.
All inputs are finite; a program needn't handle non-finite values.
Results may differ from the reference program's by a relative error of at most 0.005.
The reference program's roundings to bfloat16 on the way (of `q_rot`, `k_rot`, `expo` and `attended`) count: a program that leaves them out, or rounds other values in their place, can miss the bound.
Values may be sent and summed in bfloat16 or wider, within the bound.
A program may use at most 64 MiB of HBM per device.

```python
import math
import jax
import jax.numpy as jnp
import numpy as np
from jax import lax

D = 8192
HQ = 32
KVH = 8
HD = 128
TOK_DEV = 128
TOKENS = 1024
MOST = 512
DOCS = 8


def paired_draw(key):
    base_key = jax.random.fold_in(key, 29)
    key_query, key_key = jax.random.split(base_key, 2)
    queries = jnp.clip(jax.random.normal(key_query, (TOKENS, HQ * HD), jnp.float32), -6.0, 6.0)
    key_rows = jnp.clip(jax.random.normal(key_key, (TOKENS, KVH * HD), jnp.float32), -6.0, 6.0)
    return (queries, key_rows)


def draw_queries(key, part):
    return paired_draw(key)[0].astype(jnp.bfloat16)


def draw_key_proj(key, part):
    return paired_draw(key)[1].astype(jnp.bfloat16)


def block_levels(rng, dims, cuts, smallest, largest):
    gain, own = 1.0, jax.random.fold_in(rng, 6)
    for dim, blocks in cuts:
        steps = jnp.exp(jax.random.uniform(jax.random.fold_in(own, dim), (blocks,), jnp.float32, smallest / len(cuts), largest / len(cuts)))
        gain = gain * jnp.repeat(steps, dims[dim] // blocks).reshape([-1 if axis == dim else 1 for axis in range(len(dims))])
    return gain


def length_profile(count, total, bound, lean):
    weights = [(1 << 20) // math.isqrt(standing ** lean) + 1 for standing in range(2, count + 1)]
    rest, given = total - bound - (count - 1), [1] * (count - 1)
    while rest > 0:
        movable = [i for i in range(count - 1) if given[i] < bound]
        mass, remaining = sum([weights[i] for i in movable]), rest
        for i in movable:
            extra = min(bound - given[i], max(1, remaining * weights[i] // mass), rest)
            given[i] = given[i] + extra
            rest = rest - extra
    return np.array([bound] + given)


def ragged(own_key, number_of, total, limit, lean):
    if number_of == 2:
        one = jax.random.randint(own_key, (), max(1, total - limit), min(limit, total - 1) + 1)
        return jnp.stack([one, total - one])
    sizes = jnp.asarray(length_profile(number_of, total, limit, lean), jnp.int32)
    couples = (number_of - 1) // 2
    giver, taker = sizes[1:1 + 2 * couples:2], sizes[2:2 + 2 * couples:2]
    margin = jnp.minimum(giver - 1, limit - taker)
    moved = jax.random.randint(jax.random.fold_in(own_key, 1), (couples,), 0, 1 << 20) % (margin + 1)
    sizes = sizes.at[1:1 + 2 * couples:2].set(giver - moved).at[2:2 + 2 * couples:2].set(taker + moved)
    return sizes[jax.random.permutation(jax.random.fold_in(own_key, 2), number_of)]


def noise(stream_key, dims, deviation, limit, cuts=(), kind=jnp.bfloat16):
    result = jax.random.normal(stream_key, dims, jnp.float32) * deviation
    if len(cuts) > 0:
        result = block_levels(stream_key, dims, cuts, -0.22, 0.18) * result
    return jnp.clip(result, min=-limit, max=limit).astype(kind)


def setup_inputs(seed: int = 0) -> dict:
    key_of = jax.random.split(jax.random.key(seed), 6)
    return {
        "queries": draw_queries(jax.random.fold_in(key_of[5], 71), 0),
        "key_proj": draw_key_proj(jax.random.fold_in(key_of[5], 71), 0),
        "value_proj": noise(key_of[2], (TOKENS, KVH * HD), 1.0, 6.0, ((0, 8), (1, 4))),
        "lengths": ragged(key_of[3], DOCS, TOKENS, MOST, 2).astype(jnp.int32),
        "out_weight": noise(key_of[4], (HQ * HD, D), (HQ * HD) ** -0.5, 0.09375, ((1, 4),)),
    }


rope_theta = 500000.0

def doc_starts(lengths, positions):
    doc_ends = jnp.cumsum(lengths)
    picked = jnp.where(doc_ends[None, :] <= positions[:, None], lengths[None, :], 0)
    return lax.optimization_barrier(jnp.sum(picked, axis=1)).astype(jnp.int32)

def rotary(projected, offsets, head_dim):
    token_count = projected.shape[0]
    heads_grid = projected.astype(jnp.float32).reshape(token_count, -1, head_dim)
    half_dim = head_dim // 2
    inverse = rope_theta ** (-2.0 * jnp.arange(half_dim).astype(jnp.float32) / head_dim)
    angles = offsets.astype(jnp.float32)[:, None] * inverse[None, :]
    cosine = jnp.cos(angles)[:, None, :]
    sine_part = jnp.sin(angles)[:, None, :]
    first_half = heads_grid[..., :half_dim]
    second_half = heads_grid[..., half_dim:]
    rotated = jnp.concatenate([first_half * cosine - second_half * sine_part, second_half * cosine + first_half * sine_part], axis=-1)
    return rotated.reshape(token_count, -1).astype(jnp.bfloat16)

def reference(queries, key_proj, value_proj, lengths, out_weight):
    positions = jnp.arange(TOKENS, dtype=jnp.int32)
    starts = doc_starts(lengths, positions)
    offsets = positions - starts
    q_rot = rotary(queries, offsets, HD)
    k_rot = rotary(key_proj, offsets, HD)
    query_group = HQ // KVH
    window = min(MOST + TOK_DEV, TOKENS)
    blocks = TOKENS // TOK_DEV

    def one_block(block_index):
        q_begin = (block_index * TOK_DEV).astype(jnp.int32)
        k_begin = jnp.clip(q_begin - MOST, 0, TOKENS - window).astype(jnp.int32)
        q_block = lax.dynamic_slice_in_dim(q_rot, q_begin, TOK_DEV, 0).reshape(TOK_DEV, KVH, query_group, HD)
        k_block = lax.dynamic_slice_in_dim(k_rot, k_begin, window, 0).reshape(window, KVH, HD)
        v_block = lax.dynamic_slice_in_dim(value_proj, k_begin, window, 0).reshape(window, KVH, HD)
        q_pos = q_begin + jnp.arange(TOK_DEV, dtype=jnp.int32)
        k_pos = k_begin + jnp.arange(window, dtype=jnp.int32)
        q_doc = lax.dynamic_slice_in_dim(starts, q_begin, TOK_DEV, 0)
        allowed = (k_pos[None, :] <= q_pos[:, None]) & (k_pos[None, :] >= q_doc[:, None])

        def one_head(head_index):
            q_head = jnp.take(q_block, head_index, axis=1).astype(jnp.float32)
            k_head = jnp.take(k_block, head_index, axis=1).astype(jnp.float32)
            v_head = jnp.take(v_block, head_index, axis=1).astype(jnp.float32)
            scores = jnp.einsum('tgd,nd->gtn', q_head, k_head) / jnp.sqrt(jnp.float32(HD))
            scores = jnp.where(allowed[None], scores, -jnp.inf)
            row_max = lax.optimization_barrier(jnp.max(scores, axis=-1, keepdims=True))
            expo = jnp.exp(scores - row_max)
            row_sum = lax.optimization_barrier(jnp.sum(expo, axis=-1, keepdims=True))
            rounded = lax.optimization_barrier(expo.astype(jnp.bfloat16)).astype(jnp.float32)
            weighted = jnp.einsum('gtn,nd->gtd', rounded, v_head) / row_sum
            return jnp.transpose(weighted, (1, 0, 2))
        per_head = lax.map(one_head, jnp.arange(KVH, dtype=jnp.int32))
        return jnp.transpose(per_head, (1, 0, 2, 3)).reshape(TOK_DEV, HQ * HD).astype(jnp.bfloat16)
    attended = lax.map(one_block, jnp.arange(blocks, dtype=jnp.int32)).reshape(TOKENS, HQ * HD)
    return jnp.dot(attended, out_weight, preferred_element_type=jnp.float32).astype(jnp.bfloat16)
```

```python
import functools

import jax
import jax.numpy as jnp
from jax import lax
from jax.experimental import pallas as pl
from jax.experimental.pallas import tpu as pltpu
from jax.sharding import PartitionSpec as P

HD = 128
ROPE_THETA = 500000.0
MESH = pl.DeviceIdType.MESH


def kernel(
    n, heads, window, lengths, inverse, q_in, k_in, v_in, w_hbm, out,
    kv, q_rot, att, w, acc,
    w_sem, z_send, y_send, kv_recv, x_send, s_send, r_send, att_recv,
):
    tok = q_in.shape[0]
    groups = k_in.shape[1] // HD
    per = q_in.shape[1] // k_in.shape[1]
    wide = per * HD
    steps = window // 2
    chips = heads // 2
    ctx, head = lax.axis_index("ctx"), lax.axis_index("head")
    col, core = lax.rem(ctx, 2), lax.rem(head, 2)
    chip = head // 2
    partner = ctx + 1 - 2 * col
    sibling = head + 1 - 2 * core

    barrier = pltpu.get_barrier_semaphore()

    def greet(c, h):
        pl.semaphore_signal(barrier, inc=1, device_id=(c, h), device_id_type=MESH)

    expected = jnp.int32(2 + chips - 1)
    greet(partner, head)
    greet(ctx, sibling)
    for s in range(1, chips):
        greet(ctx, lax.rem(chip + s, chips) * 2 + core)
    for k in range(1, steps + 1):
        up, down = ctx + 2 * k < n, ctx - 2 * k >= 0
        expected = expected + up.astype(jnp.int32) + down.astype(jnp.int32)

        @pl.when(up)
        def _():
            greet(ctx + 2 * k, head)

        @pl.when(down)
        def _():
            greet(ctx - 2 * k, head)

    def weight_copy(h, g):
        piece = h * groups + g
        rows = pl.ds(pl.multiple_of(piece * wide, wide), wide)
        return pltpu.make_async_copy(w_hbm.at[rows, :], w.at[piece], w_sem.at[piece])

    order = []
    for s in range(chips):
        order.append(lax.rem(chip + s, chips) * 2 + core)
    for s in range(chips):
        order.append(lax.rem(chip + s, chips) * 2 + 1 - core)
    for h in order:
        for g in range(groups):
            weight_copy(h, g).start()

    pos = ctx * tok + lax.broadcasted_iota(jnp.int32, (tok, HD), 0)
    starts = jnp.zeros((tok, HD), jnp.int32)
    end = jnp.int32(0)
    for j in range(lengths.shape[0]):
        end = end + lengths[j]
        starts = jnp.where(pos >= end, end, starts)
    angle = (pos - starts).astype(jnp.float32) * inverse[...]
    cosine = jnp.cos(angle)
    sine = jnp.sin(angle)
    lane = lax.broadcasted_iota(jnp.int32, (tok, HD), 1)
    sine = jnp.where(lane < HD // 2, -sine, sine)

    def rotate(x):
        x = x.astype(jnp.float32)
        return (x * cosine + pltpu.roll(x, HD // 2, 1) * sine).astype(jnp.bfloat16)

    for g in range(groups):
        cols = pl.ds(g * HD, HD)
        kv[g, 0, pl.ds(0, tok), :] = rotate(k_in[:, cols])
        kv[g, 1, pl.ds(0, tok), :] = v_in[:, cols]

    def slot(g, d):
        return kv.at[g, :, pl.ds(pl.multiple_of(d * tok, tok), tok), :]

    def z_copy(k, g):
        return pltpu.make_async_remote_copy(
            src_ref=slot(g, 0), dst_ref=slot(g, 2 * k),
            send_sem=z_send.at[k - 1, g], recv_sem=kv_recv.at[2 * k, g],
            device_id=(ctx + 2 * k, head), device_id_type=MESH,
        )

    def y_copy(m, g):
        return pltpu.make_async_remote_copy(
            src_ref=slot(g, 2 * m + 2 * col), dst_ref=slot(g, 2 * m + 1),
            send_sem=y_send.at[m, g], recv_sem=kv_recv.at[2 * m + 1, g],
            device_id=(partner, head), device_id_type=MESH,
        )

    pl.semaphore_wait(barrier, expected)

    for g in range(groups):
        for k in range(1, steps + 1):

            @pl.when(ctx + 2 * k < n)
            def _():
                z_copy(k, g).start()

        @pl.when(col == 0)
        def _():
            y_copy(0, g).start()

    for d in range(1, window + 1):

        @pl.when(ctx < d)
        def _():
            for g in range(groups):
                kv[g, :, pl.ds(d * tok, tok), :] = jnp.zeros((2, tok, HD), jnp.bfloat16)

    for j in range(groups * per):
        g, r = divmod(j, per)
        q_rot[g, pl.ds(r * tok, tok), :] = rotate(q_in[:, pl.ds(j * HD, HD)])

    def relay(g):
        for k in range(1, steps + 1):

            @pl.when(ctx - 2 * k >= 0)
            def _():
                z_copy(k, g).wait_recv()

            if k <= steps - 1:

                @pl.when((col == 0) & (ctx - 2 * k >= 0))
                def _():
                    y_copy(k, g).start()

            @pl.when((col == 1) & (ctx - 2 * k >= 0))
            def _():
                y_copy(k - 1, g).start()

    keys = (window + 1) * tok
    spot = lax.broadcasted_iota(jnp.int32, (tok, keys), 1)
    back = spot // tok
    key_pos = (ctx - back) * tok + (spot - back * tok)
    allowed = (key_pos <= pos[:, :1]) & (key_pos >= starts[:, :1])
    scale = jnp.float32(HD ** -0.5)

    def attend(g):
        for m in range(steps):

            @pl.when(ctx - 2 * m - 1 >= 0)
            def _():
                y_copy(m, g).wait_recv()

        scores = lax.dot_general(
            q_rot[g], kv[g, 0], (((1,), (1,)), ((), ())), preferred_element_type=jnp.float32
        )
        for r in range(per):
            one = jnp.where(allowed, scores[r * tok:(r + 1) * tok] * scale, -1e30)
            expo = jnp.exp(one - jnp.max(one, axis=-1, keepdims=True))
            total = jnp.sum(expo, axis=-1, keepdims=True)
            mixed = jnp.dot(
                expo.astype(jnp.bfloat16), kv[g, 1], preferred_element_type=jnp.float32
            )
            att[head, g, :, pl.ds(r * HD, HD)] = (mixed / total).astype(jnp.bfloat16)

    def x_copy(s, g):
        return pltpu.make_async_remote_copy(
            src_ref=att.at[head, g], dst_ref=att.at[head, g],
            send_sem=x_send.at[s - 1, g], recv_sem=att_recv.at[head, g],
            device_id=(ctx, lax.rem(chip + s, chips) * 2 + core), device_id_type=MESH,
        )

    def core_copy(h, g, sem):
        return pltpu.make_async_remote_copy(
            src_ref=att.at[h, g], dst_ref=att.at[h, g],
            send_sem=sem, recv_sem=att_recv.at[h, g],
            device_id=(ctx, sibling), device_id_type=MESH,
        )

    def arrived(h, g):
        core_copy(h, g, s_send.at[g]).wait_recv()

    def share(g):
        for s in range(1, chips):
            x_copy(s, g).start()
        core_copy(head, g, s_send.at[g]).start()

    def project(h, g, first=False):
        weight_copy(h, g).wait()
        part = jnp.dot(att[h, g], w[h * groups + g], preferred_element_type=jnp.float32)
        acc[...] = part if first else acc[...] + part

    relay(0)
    for g in range(groups):
        if g + 1 < groups:
            relay(g + 1)
        attend(g)
        share(g)
    for g in range(groups):
        project(head, g, first=g == 0)
    for g in range(groups):
        arrived(sibling, g)
        project(sibling, g)
    for g in range(groups):
        for s in range(1, chips):
            h = order[s]
            arrived(h, g)
            core_copy(h, g, r_send.at[s - 1, g]).start()
            project(h, g)
        for s in range(1, chips):
            h = order[chips + s]
            arrived(h, g)
            project(h, g)
    out[...] = acc[...].astype(out.dtype)

    for g in range(groups):
        for k in range(1, steps + 1):

            @pl.when(ctx + 2 * k < n)
            def _():
                z_copy(k, g).wait_send()

        for m in range(steps):

            @pl.when(ctx - 2 * m - 2 * col >= 0)
            def _():
                y_copy(m, g).wait_send()

        for s in range(1, chips):
            x_copy(s, g).wait_send()
            core_copy(order[s], g, r_send.at[s - 1, g]).wait_send()
        core_copy(head, g, s_send.at[g]).wait_send()


def on_device(n, heads, queries, key_proj, value_proj, lengths, out_weight):
    tok = queries.shape[0]
    groups = key_proj.shape[1] // HD
    wide = queries.shape[1] // groups
    columns = out_weight.shape[1]
    window = n // 2
    half = -2.0 * jnp.arange(HD // 2).astype(jnp.float32) / HD
    inverse = ROPE_THETA ** half
    inverse = jnp.concatenate([inverse, inverse])[None, :]
    vmem = pl.BlockSpec(memory_space=pltpu.VMEM)
    dma = pltpu.SemaphoreType.DMA
    return pl.pallas_call(
        functools.partial(kernel, n, heads, window),
        out_shape=jax.ShapeDtypeStruct((tok, columns), jnp.bfloat16),
        in_specs=[
            pl.BlockSpec(memory_space=pltpu.SMEM), vmem, vmem, vmem, vmem,
            pl.BlockSpec(memory_space=pl.ANY),
        ],
        out_specs=vmem,
        scratch_shapes=[
            pltpu.VMEM((groups, 2, (window + 1) * tok, HD), jnp.bfloat16),
            pltpu.VMEM((groups, wide // HD * tok, HD), jnp.bfloat16),
            pltpu.VMEM((heads, groups, tok, wide), jnp.bfloat16),
            pltpu.VMEM((heads * groups, wide, columns), jnp.bfloat16),
            pltpu.VMEM((tok, columns), jnp.float32),
            dma((heads * groups,)),
            dma((window // 2, groups)),
            dma((window // 2, groups)),
            dma((window + 1, groups)),
            dma((heads // 2, groups)),
            dma((groups,)),
            dma((heads // 2, groups)),
            dma((heads, groups)),
        ],
        compiler_params=pltpu.CompilerParams(
            collective_id=0, has_side_effects=True, vmem_limit_bytes=50 * 2**20
        ),
    )(lengths, inverse, queries, key_proj, value_proj, out_weight)


def solution(mesh):
    placed = (P("ctx", "head"), P("ctx", "head"), P("ctx", "head"), P(), P(None, "head"))
    return jax.shard_map(
        functools.partial(on_device, mesh.shape["ctx"], mesh.shape["head"]),
        mesh=mesh, in_specs=placed, out_specs=P("ctx", "head"), check_vma=False,
    )
```

```python
import functools

import jax
import jax.numpy as jnp
from jax import lax
from jax.experimental import pallas as pl
from jax.experimental.pallas import tpu as pltpu
from jax.sharding import PartitionSpec as P

HD = 128
ROPE_THETA = 500000.0
MESH = pl.DeviceIdType.MESH


def kernel(
    n, heads, window, lengths_hbm, inverse_hbm, q_hbm, k_hbm, v_hbm, w_hbm, out,
    lengths, inverse, q_in, k_in, kv, q_rot, att, w, acc,
    in_sem, v_sem, w_sem, z_send, y_send, kv_recv, x_send, s_send, r_send, att_recv,
):
    tok = q_in.shape[0]
    groups = k_in.shape[1] // HD
    per = q_in.shape[1] // k_in.shape[1]
    wide = per * HD
    steps = window // 2
    parts = 2 * groups
    chips = heads // 2
    ctx, head = lax.axis_index("ctx"), lax.axis_index("head")
    col, core = lax.rem(ctx, 2), lax.rem(head, 2)
    chip = head // 2
    partner = ctx + 1 - 2 * col
    sibling = head + 1 - 2 * core

    barrier = pltpu.get_barrier_semaphore()

    def greet(c, h):
        pl.semaphore_signal(barrier, inc=1, device_id=(c, h), device_id_type=MESH)

    expected = jnp.int32(2 + chips - 1)
    greet(partner, head)
    greet(ctx, sibling)
    for s in range(1, chips):
        greet(ctx, lax.rem(chip + s, chips) * 2 + core)
    up, down = ctx + 2 < n, ctx - 2 >= 0
    expected = expected + up.astype(jnp.int32) + down.astype(jnp.int32)

    @pl.when(up)
    def _():
        greet(ctx + 2, head)

    @pl.when(down)
    def _():
        greet(ctx - 2, head)

    own = [
        pltpu.make_async_copy(src, dst, in_sem.at[i])
        for i, (src, dst) in enumerate(
            [(lengths_hbm, lengths), (inverse_hbm, inverse), (k_hbm, k_in), (q_hbm, q_in)]
        )
    ]
    values = [
        pltpu.make_async_copy(
            v_hbm.at[:, pl.ds(g * HD, HD)], kv.at[g, 1, pl.ds(0, tok), :], v_sem.at[g]
        )
        for g in range(groups)
    ]
    for copy in own[:3] + values + own[3:]:
        copy.start()

    def weight_copy(h, g):
        piece = h * groups + g
        rows = pl.ds(pl.multiple_of(piece * wide, wide), wide)
        return pltpu.make_async_copy(w_hbm.at[rows, :], w.at[piece], w_sem.at[piece])

    order = []
    for s in range(chips):
        order.append(lax.rem(chip + s, chips) * 2 + core)
    for s in range(chips):
        order.append(lax.rem(chip + s, chips) * 2 + 1 - core)
    own[0].wait()
    own[1].wait()
    pos = ctx * tok + lax.broadcasted_iota(jnp.int32, (tok, HD), 0)
    starts = jnp.zeros((tok, HD), jnp.int32)
    end = jnp.int32(0)
    for j in range(lengths.shape[0]):
        end = end + lengths[j]
        starts = jnp.where(pos >= end, end, starts)
    angle = (pos - starts).astype(jnp.float32) * inverse[...]
    cosine = jnp.cos(angle)
    sine = jnp.sin(angle)
    lane = lax.broadcasted_iota(jnp.int32, (tok, HD), 1)
    sine = jnp.where(lane < HD // 2, -sine, sine)

    def rotate(x):
        x = x.astype(jnp.float32)
        return (x * cosine + pltpu.roll(x, HD // 2, 1) * sine).astype(jnp.bfloat16)

    own[2].wait()
    for g in range(groups):
        kv[g, 0, pl.ds(0, tok), :] = rotate(k_in[:, pl.ds(g * HD, HD)])
        values[g].wait()

    def slot(g, d):
        return kv.at[g, :, pl.ds(pl.multiple_of(d * tok, tok), tok), :]

    def z_copy(k, g):
        return pltpu.make_async_remote_copy(
            src_ref=slot(g, 2 * k - 2), dst_ref=slot(g, 2 * k),
            send_sem=z_send.at[k - 1, g], recv_sem=kv_recv.at[2 * k, g],
            device_id=(ctx + 2, head), device_id_type=MESH,
        )

    def y_copy(m, g):
        return pltpu.make_async_remote_copy(
            src_ref=slot(g, 2 * m + 2 * col), dst_ref=slot(g, 2 * m + 1),
            send_sem=y_send.at[m, g], recv_sem=kv_recv.at[2 * m + 1, g],
            device_id=(partner, head), device_id_type=MESH,
        )

    pl.semaphore_wait(barrier, expected)

    for g in range(groups):

        @pl.when(up)
        def _():
            z_copy(1, g).start()

        @pl.when(col == 0)
        def _():
            y_copy(0, g).start()

    for h in order:
        for g in range(groups):
            weight_copy(h, g).start()

    for d in range(1, window + 1):

        @pl.when(ctx < d)
        def _():
            for g in range(groups):
                kv[g, :, pl.ds(d * tok, tok), :] = jnp.zeros((2, tok, HD), jnp.bfloat16)

    own[3].wait()
    for j in range(groups * per):
        g, r = divmod(j, per)
        q_rot[g, pl.ds(r * tok, tok), :] = rotate(q_in[:, pl.ds(j * HD, HD)])

    def relay(k, g):
        here = ctx - 2 * k >= 0

        @pl.when(here)
        def _():
            z_copy(k, g).wait_recv()

        if k < steps:

            @pl.when(here & up)
            def _():
                z_copy(k + 1, g).start()

            @pl.when(here & (col == 0))
            def _():
                y_copy(k, g).start()

        @pl.when(here & (col == 1))
        def _():
            y_copy(k - 1, g).start()

    keys = (window + 1) * tok
    spot = lax.broadcasted_iota(jnp.int32, (tok, keys), 1)
    back = spot // tok
    key_pos = (ctx - back) * tok + (spot - back * tok)
    allowed = (key_pos <= pos[:, :1]) & (key_pos >= starts[:, :1])
    scale = jnp.float32(HD ** -0.5)

    def attend(g):
        for m in range(steps):

            @pl.when(ctx - 2 * m - 1 >= 0)
            def _():
                y_copy(m, g).wait_recv()

        scores = lax.dot_general(
            q_rot[g], kv[g, 0], (((1,), (1,)), ((), ())), preferred_element_type=jnp.float32
        )
        for r in range(per):
            one = jnp.where(allowed, scores[r * tok:(r + 1) * tok] * scale, -1e30)
            expo = jnp.exp(one - jnp.max(one, axis=-1, keepdims=True))
            total = jnp.sum(expo, axis=-1, keepdims=True)
            mixed = jnp.dot(
                expo.astype(jnp.bfloat16), kv[g, 1], preferred_element_type=jnp.float32
            )
            p, place = divmod(r, per // 2)
            att[head, 2 * g + p, :, pl.ds(place * HD, HD)] = (mixed / total).astype(jnp.bfloat16)
            if place == per // 2 - 1:
                share(2 * g + p)

    def x_copy(s, g):
        return pltpu.make_async_remote_copy(
            src_ref=att.at[head, g], dst_ref=att.at[head, g],
            send_sem=x_send.at[s - 1, g], recv_sem=att_recv.at[head, g],
            device_id=(ctx, lax.rem(chip + s, chips) * 2 + core), device_id_type=MESH,
        )

    def core_copy(h, g, sem):
        return pltpu.make_async_remote_copy(
            src_ref=att.at[h, g], dst_ref=att.at[h, g],
            send_sem=sem, recv_sem=att_recv.at[h, g],
            device_id=(ctx, sibling), device_id_type=MESH,
        )

    def arrived(h, g):
        core_copy(h, g, s_send.at[g]).wait_recv()

    def share(g):
        for s in range(1, chips):
            x_copy(s, g).start()
        core_copy(head, g, s_send.at[g]).start()

    def project(h, b, first=False):
        if b % 2 == 0:
            weight_copy(h, b // 2).wait()
        rows = w[h * groups + b // 2, pl.ds(b % 2 * (wide // 2), wide // 2), :]
        part = jnp.dot(att[h, b], rows, preferred_element_type=jnp.float32)
        acc[...] = part if first else acc[...] + part

    for k in range(1, steps + 1):
        for g in range(groups):
            relay(k, g)
    for g in range(groups):
        attend(g)
    def forward(b):
        for s in range(1, chips):
            arrived(order[s], b)
            core_copy(order[s], b, r_send.at[s - 1, b]).start()

    for b in range(parts):
        project(head, b, first=b == 0)
    for b in range(parts):
        arrived(sibling, b)
        project(sibling, b)
    forward(0)
    for b in range(parts):
        for s in range(1, chips):
            project(order[s], b)
        if b + 1 < parts:
            forward(b + 1)
        for s in range(1, chips):
            h = order[chips + s]
            arrived(h, b)
            project(h, b)
    out[...] = acc[...].astype(out.dtype)

    for g in range(groups):
        for k in range(1, steps + 1):

            @pl.when(up & (ctx - 2 * k + 2 >= 0))
            def _():
                z_copy(k, g).wait_send()

        for m in range(steps):

            @pl.when(ctx - 2 * m - 2 * col >= 0)
            def _():
                y_copy(m, g).wait_send()

    for b in range(parts):
        for s in range(1, chips):
            x_copy(s, b).wait_send()
            core_copy(order[s], b, r_send.at[s - 1, b]).wait_send()
        core_copy(head, b, s_send.at[b]).wait_send()


def on_device(n, heads, queries, key_proj, value_proj, lengths, out_weight):
    tok = queries.shape[0]
    groups = key_proj.shape[1] // HD
    wide = queries.shape[1] // groups
    columns = out_weight.shape[1]
    window = n // 2
    half = -2.0 * jnp.arange(HD // 2).astype(jnp.float32) / HD
    inverse = ROPE_THETA ** half
    inverse = jnp.concatenate([inverse, inverse])[None, :]
    vmem = pl.BlockSpec(memory_space=pltpu.VMEM)
    dma = pltpu.SemaphoreType.DMA
    return pl.pallas_call(
        functools.partial(kernel, n, heads, window),
        out_shape=jax.ShapeDtypeStruct((tok, columns), jnp.bfloat16),
        in_specs=[pl.BlockSpec(memory_space=pltpu.HBM)] * 6,
        out_specs=vmem,
        scratch_shapes=[
            pltpu.SMEM(lengths.shape, jnp.int32),
            pltpu.VMEM(inverse.shape, jnp.float32),
            pltpu.VMEM(queries.shape, jnp.bfloat16),
            pltpu.VMEM(key_proj.shape, jnp.bfloat16),
            pltpu.VMEM((groups, 2, (window + 1) * tok, HD), jnp.bfloat16),
            pltpu.VMEM((groups, wide // HD * tok, HD), jnp.bfloat16),
            pltpu.VMEM((heads, 2 * groups, tok, wide // 2), jnp.bfloat16),
            pltpu.VMEM((heads * groups, wide, columns), jnp.bfloat16),
            pltpu.VMEM((tok, columns), jnp.float32),
            dma((4,)),
            dma((groups,)),
            dma((heads * groups,)),
            dma((window // 2, groups)),
            dma((window // 2, groups)),
            dma((window + 1, groups)),
            dma((heads // 2, 2 * groups)),
            dma((2 * groups,)),
            dma((heads // 2, 2 * groups)),
            dma((heads, 2 * groups)),
        ],
        compiler_params=pltpu.CompilerParams(
            collective_id=0, has_side_effects=True, vmem_limit_bytes=63 * 2**20
        ),
    )(lengths, inverse, queries, key_proj, value_proj, out_weight)


def solution(mesh):
    placed = (P("ctx", "head"), P("ctx", "head"), P("ctx", "head"), P(), P(None, "head"))
    return jax.shard_map(
        functools.partial(on_device, mesh.shape["ctx"], mesh.shape["head"]),
        mesh=mesh, in_specs=placed, out_specs=P("ctx", "head"), check_vma=False,
    )
```
